128 devices in a mesh: morton: 128 (over y, z, x, core).
Axes of the slice: x: 4, y: 4, z: 4, core: 2. Of those that a mesh axis runs over, the one named last changes fastest.
Arguments:
- multipoles: bfloat16 [3, 488, 32768], P(None, None, 'morton'), may hold values from -6 to 6
- upward_ops: bfloat16 [8, 488, 488], replicated, may hold values from -0.25 to 0.25
- transfer_ops: bfloat16 [36, 488, 488], replicated, may hold values from -0.25 to 0.25
- live_counts: int32 [128], P('morton'), may hold values from 128 to 256, as said below
- seam_joins: int32 [128, 2], P('morton'), may hold values from 0 to 1, as said below
- send_slots: int32 [128, 1024], P('morton'), may hold values from 0 to 127
- vlist_cols: int32 [32768, 36], P('morton'), may hold values from 0 to 1280, as said below
Outputs:
- local_check: float32 [3, 488, 32768], P(None, None, 'morton')
- parent_mult: float32 [3, 488, 4096], P(None, None, 'morton')
The draws below stay inside these ranges and needn't reach their ends.
Inputs may be any that keep to these rules, and one draw needn't show every extreme that they name: `live_counts`: some device has 256 boxes in use and some has 128. seam_joins[d, 0] equals seam_joins[d - 1, 1]; the first device's left entry and the last device's right entry are 0; the seam between the first two devices and the seam between the last two are always joined. `vlist_cols`: entries below 256 are the device's own slots, entries from 256 below 1280 are received ghost columns, and 1280 marks an absent source; every device uses every ghost column.
All inputs are finite; a program needn't handle non-finite values.
Results may differ from the reference program's by a relative error of at most 0.0003.
Values may be sent and summed in bfloat16 or wider, within the bound.
No kernel may reach another device: no remote copies, remote signals or barrier semaphores. Data moves between devices by JAX's collectives and lax.ppermute only.
A program may use at most 192 MiB of HBM per device.

```python
import jax
import jax.numpy as jnp
from jax import lax

CHAN = 3
NEQ = 488
REL = 36
SLOT = 256
GHOST = 8
BOXES = 32768
N_MORTON = 128


def draw_live_counts(key, part):
    key = jax.random.fold_in(key, 11)
    first_key, second_key = jax.random.split(key)
    counts = jax.random.randint(first_key, (N_MORTON,), SLOT // 2, SLOT + 1)
    picks = jax.random.permutation(second_key, N_MORTON)
    counts = counts.at[picks[0]].set(SLOT).at[picks[1]].set(SLOT // 2)
    return counts.astype(jnp.int32)


def draw_seam_joins(key, part):
    key = jax.random.fold_in(key, 12)
    levels = jax.random.randint(key, (N_MORTON - 1,), 0, 4)
    bounds = (levels >= 1).astype(jnp.int32)
    bounds = bounds.at[0].set(1).at[N_MORTON - 2].set(1)
    zero_entry = jnp.zeros((1,), jnp.int32)
    left_side = jnp.concatenate([zero_entry, bounds])
    right_side = jnp.concatenate([bounds, zero_entry])
    return jnp.stack([left_side, right_side], axis=1).astype(jnp.int32)


def draw_vlist_cols(key, part):
    key = jax.random.fold_in(key, 13)
    kind_key, local_key, shift_key = jax.random.split(key, 3)
    ghost_cols = N_MORTON * GHOST
    kinds = jax.random.randint(kind_key, (N_MORTON, SLOT * REL), 0, 5)
    local = jax.random.randint(local_key, (N_MORTON, SLOT * REL), 0, SLOT)
    shifts = jax.random.randint(shift_key, (N_MORTON, 1), 0, ghost_cols)
    is_remote = (kinds >= 2).astype(jnp.int32)
    ranks = jnp.cumsum(is_remote, axis=1) - is_remote
    remote = SLOT + (ranks + shifts) % ghost_cols
    empty = SLOT + ghost_cols
    values = jnp.where(kinds == 0, local, jnp.where(kinds == 1, empty, remote))
    values = values.reshape(N_MORTON * SLOT, REL)
    values = values.at[0, 0].set(empty)
    return values.astype(jnp.int32)


def set_ends(entries, rng, smallest, high):
    spot = [jax.random.randint(jax.random.fold_in(rng, axis), (), 0, length) for axis, length in enumerate(entries.shape)]
    longest = entries.shape.index(max(entries.shape))
    next_to = spot[:longest] + [(spot[longest] + 1) % entries.shape[longest]] + spot[longest + 1:]
    return entries.at[tuple(spot)].set(smallest).at[tuple(next_to)].set(high)


def level_of(rng, extent, cuts, low, top_value):
    def one(position, parts):
        steps = jax.random.uniform(jax.random.fold_in(jax.random.fold_in(rng, 6), position), (parts,), jnp.float32, low / len(cuts), top_value / len(cuts))
        return jnp.repeat(jnp.exp(steps), extent[position] // parts).reshape((-1,) + (1,) * (len(extent) - position - 1))

    gain = one(*cuts[0])
    for cut in cuts[1:]:
        gain = gain * one(*cut)
    return gain


def bell_draw(key, dims, scale, most, pieces=(), kind=jnp.bfloat16):
    result = jax.random.normal(key, dims, jnp.float32) * scale
    if len(pieces) > 0:
        result = level_of(key, dims, pieces, -0.22, 0.18) * result
    return jnp.clip(result, min=-most, max=most).astype(kind)


def setup_inputs(seed: int = 0) -> dict:
    key_list = jax.random.split(jax.random.key(seed), 8)
    multipoles = bell_draw(key_list[0], (CHAN, NEQ, BOXES), 1.0, 6.0, ((2, 128),))
    upward_ops = bell_draw(key_list[1], (8, NEQ, NEQ), NEQ ** -0.5, 0.25)
    transfer_ops = bell_draw(key_list[2], (REL, NEQ, NEQ), NEQ ** -0.5, 0.25)
    live_counts = draw_live_counts(jax.random.fold_in(key_list[7], 71), 0)
    seam_joins = draw_seam_joins(jax.random.fold_in(key_list[7], 71), 0)
    send_slots = set_ends(jax.random.randint(key_list[5], (N_MORTON, N_MORTON * GHOST), 0, SLOT // 2), jax.random.fold_in(key_list[5], 1), 0, (SLOT // 2) - 1).astype(jnp.int32)
    vlist_cols = draw_vlist_cols(jax.random.fold_in(key_list[7], 71), 0)
    return {"multipoles": multipoles, "upward_ops": upward_ops, "transfer_ops": transfer_ops, "live_counts": live_counts, "seam_joins": seam_joins, "send_slots": send_slots, "vlist_cols": vlist_cols}


def reference(multipoles, upward_ops, transfer_ops, live_counts, seam_joins, send_slots, vlist_cols):
    dev_count = N_MORTON
    group_total = SLOT // 8
    slot_ids = jnp.arange(SLOT, dtype=jnp.int32)
    alive = (slot_ids[None, :] < live_counts[:, None]).reshape(-1)
    masked = jnp.where(alive[None, None, :], multipoles, jnp.zeros_like(multipoles))
    children = masked.astype(jnp.float32).reshape(CHAN, NEQ, dev_count * group_total, 8)
    partial_value = jnp.einsum('oij,cjgo->cig', upward_ops.astype(jnp.float32), children)
    partial_value = partial_value.reshape(CHAN, NEQ, dev_count, group_total)
    last_group = ((live_counts - 1) // 8).astype(jnp.int32)
    group_ids = jnp.arange(group_total, dtype=jnp.int32)
    onehot = group_ids[None, :] == last_group[:, None]
    firsts = partial_value[:, :, :, 0]
    last_parts = jnp.sum(jnp.where(onehot[None, None], partial_value, jnp.float32(0.0)), axis=3)
    zero_column = jnp.zeros((CHAN, NEQ, 1), jnp.float32)
    left_last = jnp.concatenate([zero_column, last_parts[:, :, :-1]], axis=2)
    right_first = jnp.concatenate([firsts[:, :, 1:], zero_column], axis=2)
    join_left = seam_joins[:, 0].astype(jnp.float32)
    join_right = seam_joins[:, 1].astype(jnp.float32)
    first_mask = (group_ids == 0)[None, None, None, :]
    parent_mult = partial_value + jnp.where(first_mask, (join_left[None, None, :] * left_last)[..., None], jnp.float32(0.0))
    parent_mult = parent_mult + jnp.where(onehot[None, None], (join_right[None, None, :] * right_first)[..., None], jnp.float32(0.0))
    parent_mult = parent_mult.reshape(CHAN, NEQ, dev_count * group_total)

    ghost_ids = jnp.arange(dev_count * GHOST, dtype=jnp.int32)
    source_dev = ghost_ids // GHOST
    ghost_pos = ghost_ids % GHOST
    operators = transfer_ops.astype(jnp.float32)

    def one_device(device):
        local = lax.dynamic_slice_in_dim(masked, device * SLOT, SLOT, 2)
        picked = send_slots[source_dev, device * GHOST + ghost_pos]
        remote = jnp.take(masked, (source_dev * SLOT + picked).astype(jnp.int32), axis=2)
        buffer = jnp.concatenate([local, remote, jnp.zeros((CHAN, NEQ, 1), multipoles.dtype)], axis=2)
        targets = lax.dynamic_slice_in_dim(vlist_cols, device * SLOT, SLOT, 0)
        columns = jnp.take(buffer, targets.T, axis=2).astype(jnp.float32)
        values = jnp.einsum('rij,cjrb->cib', operators, columns)
        keep = slot_ids < live_counts[device]
        return jnp.where(keep[None, None, :], values, jnp.float32(0.0))

    per_device = lax.map(one_device, jnp.arange(dev_count, dtype=jnp.int32))
    local_check = jnp.transpose(per_device, (1, 2, 0, 3)).reshape(CHAN, NEQ, dev_count * SLOT)
    return local_check, parent_mult
```

```python
import functools

import jax
import jax.numpy as jnp
from jax import lax
from jax.experimental import pallas as pl
from jax.experimental.pallas import tpu as pltpu
from jax.sharding import PartitionSpec as P

BOX = 16
LANES = 128
KPAD = 512
BF16 = jnp.bfloat16
F32 = jnp.float32


def pack_kernel(mult_ref, slots_ref, out_ref):
    channels, points, send_slots = mult_ref.shape
    ghosts = slots_ref.shape[1]
    box_ids = lax.broadcasted_iota(jnp.int32, (send_slots, ghosts), 0)
    onehot = jnp.where(box_ids == slots_ref[...], 1.0, 0.0).astype(BF16)
    for c in range(channels):
        rows = lax.dot_general(
            onehot, mult_ref[c], (((0,), (1,)), ((), ())), preferred_element_type=F32
        ).astype(BF16)
        rows = jnp.concatenate([rows, jnp.zeros((ghosts, KPAD - points), BF16)], axis=1)
        out_ref[:, c * KPAD : (c + 1) * KPAD] = rows


def pack(multipoles, send_slots):
    channels, points, slots = multipoles.shape
    ghosts = send_slots.shape[1]
    half = slots // 2
    return pl.pallas_call(
        pack_kernel,
        grid=(1,),
        in_specs=[
            pl.BlockSpec((channels, points, half), lambda i: (0, 0, 0)),
            pl.BlockSpec((1, ghosts), lambda i: (0, 0)),
        ],
        out_specs=pl.BlockSpec((ghosts, channels * KPAD), lambda i: (0, 0)),
        out_shape=jax.ShapeDtypeStruct((ghosts, channels * KPAD), BF16),
        compiler_params=pltpu.CompilerParams(vmem_limit_bytes=40 * 2**20),
    )(multipoles, send_slots)


def local_kernel(live_ref, mult_ref, out_ref):
    channels, points, slots = mult_ref.shape
    keep = lax.broadcasted_iota(jnp.int32, (slots, 1), 0) < live_ref[0]
    for c in range(channels):
        rows = jnp.where(keep, mult_ref[c].astype(F32).T, 0.0).astype(BF16)
        rows = jnp.concatenate([rows, jnp.zeros((slots, KPAD - points), BF16)], axis=1)
        out_ref[:, c * KPAD : (c + 1) * KPAD] = rows


def local_rows(live, multipoles):
    channels, points, slots = multipoles.shape
    return pl.pallas_call(
        local_kernel,
        in_specs=[
            pl.BlockSpec(memory_space=pltpu.SMEM),
            pl.BlockSpec(memory_space=pltpu.VMEM),
        ],
        out_specs=pl.BlockSpec(memory_space=pltpu.VMEM),
        out_shape=jax.ShapeDtypeStruct((slots, channels * KPAD), BF16),
        compiler_params=pltpu.CompilerParams(vmem_limit_bytes=40 * 2**20),
    )(live, multipoles)


def m2l_kernel(vl_ref, live_ref, arr_ref, loc_ref, t_ref, out_ref, src, g0, g1, acc, *, rel):
    slots = loc_ref.shape[0]
    ghosts = arr_ref.shape[0]
    channels, points, _ = out_ref.shape
    chunks = KPAD // LANES
    step = pl.program_id(0)

    def gather(r, dst):
        base = r * slots
        for t in range(slots):
            i = pl.multiple_of(vl_ref[base + t], BOX)
            dst[pl.ds(t * BOX, BOX), :] = src[pl.ds(i, BOX), :]

    def apply(k, got):
        for c in range(channels):
            x = jnp.concatenate(
                [got[pl.ds(c * chunks + q, slots, stride=BOX), :].astype(BF16) for q in range(chunks)],
                axis=1,
            )
            acc[c] += jnp.dot(x, t_ref[k], preferred_element_type=F32)

    @pl.when(step == 0)
    def _():
        def fill(ref, first):
            def one(b, carry):
                rows = ref[pl.ds(pl.multiple_of(b * 8, 8), 8), :].astype(F32)
                for q in range(channels * chunks):
                    src[pl.ds((first + b * 8) * BOX + q, 8, stride=BOX), :] = rows[:, q * LANES : (q + 1) * LANES]
                return carry

            lax.fori_loop(0, ref.shape[0] // 8, one, 0, unroll=4)

        fill(loc_ref, 0)
        fill(arr_ref, slots)
        src[pl.ds((slots + ghosts) * BOX, BOX), :] = jnp.zeros((BOX, LANES), F32)
        acc[...] = jnp.zeros_like(acc)
        gather(0, g0)

    gather(2 * step + 1, g1)
    apply(0, g0)
    gather(jnp.minimum(2 * step + 2, rel - 1), g0)
    apply(1, g1)

    @pl.when(step == pl.num_programs(0) - 1)
    def _():
        keep = lax.broadcasted_iota(jnp.int32, (1, slots), 1) < live_ref[0]
        for c in range(channels):
            out_ref[c] = jnp.where(keep, acc[c].T[:points], 0.0)


def m2l(cols, live, arrived, local, ops, channels, points):
    rel = ops.shape[0]
    ghosts = arrived.shape[0]
    slots = local.shape[0]
    width = channels * KPAD
    return pl.pallas_call(
        functools.partial(m2l_kernel, rel=rel),
        grid_spec=pltpu.PrefetchScalarGridSpec(
            num_scalar_prefetch=2,
            grid=(rel // 2,),
            in_specs=[
                pl.BlockSpec((ghosts, width), lambda i, *_: (0, 0)),
                pl.BlockSpec((slots, width), lambda i, *_: (0, 0)),
                pl.BlockSpec((2, KPAD, KPAD), lambda i, *_: (i, 0, 0)),
            ],
            out_specs=pl.BlockSpec((channels, points, slots), lambda i, *_: (0, 0, 0)),
            scratch_shapes=[
                pltpu.VMEM(((slots + ghosts + 8) * BOX, LANES), F32),
                pltpu.VMEM((slots * BOX, LANES), F32),
                pltpu.VMEM((slots * BOX, LANES), F32),
                pltpu.VMEM((channels, slots, KPAD), F32),
            ],
        ),
        out_shape=jax.ShapeDtypeStruct((channels, points, slots), F32),
        compiler_params=pltpu.CompilerParams(vmem_limit_bytes=50 * 2**20),
    )(cols, live, arrived, local, ops)


def shifted(cells, step):
    count = lax.axis_size("morton")
    if step > 0:
        pairs = [(i, i + 1) for i in range(count - 1)]
    else:
        pairs = [(i + 1, i) for i in range(count - 1)]
    return lax.ppermute(cells, "morton", pairs)


def body(multipoles, upward_ops, transfer_ops, live_counts, seam_joins, send_slots, vlist_cols):
    channels, points, slot_total = multipoles.shape
    group_total = slot_total // 8
    dev_count = lax.axis_size("morton")
    ghosts = send_slots.shape[1]
    width = channels * KPAD
    outgoing = pack(multipoles, send_slots)
    outgoing, multipoles = lax.optimization_barrier((outgoing, multipoles))
    arrived = lax.all_to_all(
        outgoing.reshape(dev_count, ghosts // dev_count, width), "morton", 0, 0, tiled=True
    ).reshape(ghosts, width)

    local = local_rows(live_counts, multipoles)
    ops = jnp.pad(jnp.swapaxes(transfer_ops, 1, 2), ((0, 0), (0, KPAD - points), (0, KPAD - points)))
    cols = (vlist_cols.T * BOX).reshape(-1)

    slot_ids = jnp.arange(slot_total, dtype=jnp.int32)
    keep = (slot_ids < live_counts[0])[None, None, :]
    masked = jnp.where(keep, multipoles, jnp.zeros_like(multipoles))
    children = masked.reshape(channels, points, group_total, 8)
    partial_value = jnp.einsum("oij,cjgo->cig", upward_ops, children, preferred_element_type=F32)
    last_group = (live_counts[0] - 1) // 8
    last_part = lax.dynamic_slice_in_dim(partial_value, last_group, 1, 2)[:, :, 0]
    from_left = shifted(last_part, 1)
    from_right = shifted(partial_value[:, :, 0], -1)
    group_ids = jnp.arange(group_total, dtype=jnp.int32)
    joins = seam_joins[0].astype(F32)
    parent_mult = partial_value + jnp.where(
        (group_ids == 0)[None, None, :], (joins[0] * from_left)[:, :, None], F32(0.0)
    )
    parent_mult = parent_mult + jnp.where(
        (group_ids == last_group)[None, None, :], (joins[1] * from_right)[:, :, None], F32(0.0)
    )
    local_check = m2l(cols, live_counts, arrived, local, ops, channels, points)
    return (local_check, parent_mult)


def solution(mesh):
    placed = (
        P(None, None, "morton"),
        P(),
        P(),
        P("morton"),
        P("morton", None),
        P("morton", None),
        P("morton", None),
    )
    return jax.shard_map(
        body,
        mesh=mesh,
        in_specs=placed,
        out_specs=(P(None, None, "morton"), P(None, None, "morton")),
        check_vma=False,
    )
```

```python
import functools

import jax
import jax.numpy as jnp
from jax import lax
from jax.experimental import pallas as pl
from jax.experimental.pallas import tpu as pltpu
from jax.sharding import PartitionSpec as P

BOX = 12
LANES = 128
KPAD = 512
BF16 = jnp.bfloat16
F32 = jnp.float32


def pack_kernel(mult_ref, slots_ref, out_ref):
    channels, points, send_slots = mult_ref.shape
    ghosts = slots_ref.shape[1]
    box_ids = lax.broadcasted_iota(jnp.int32, (send_slots, ghosts), 0)
    onehot = jnp.where(box_ids == slots_ref[...], 1.0, 0.0).astype(BF16)
    for c in range(channels):
        rows = lax.dot_general(
            onehot, mult_ref[c], (((0,), (1,)), ((), ())), preferred_element_type=F32
        ).astype(BF16)
        rows = jnp.concatenate([rows, jnp.zeros((ghosts, KPAD - points), BF16)], axis=1)
        out_ref[:, c * KPAD : (c + 1) * KPAD] = rows


def pack(multipoles, send_slots):
    channels, points, slots = multipoles.shape
    ghosts = send_slots.shape[1]
    half = slots // 2
    return pl.pallas_call(
        pack_kernel,
        grid=(1,),
        in_specs=[
            pl.BlockSpec((channels, points, half), lambda i: (0, 0, 0)),
            pl.BlockSpec((1, ghosts), lambda i: (0, 0)),
        ],
        out_specs=pl.BlockSpec((ghosts, channels * KPAD), lambda i: (0, 0)),
        out_shape=jax.ShapeDtypeStruct((ghosts, channels * KPAD), BF16),
        compiler_params=pltpu.CompilerParams(vmem_limit_bytes=40 * 2**20),
    )(multipoles, send_slots)


def local_kernel(live_ref, mult_ref, out_ref):
    channels, points, slots = mult_ref.shape
    keep = lax.broadcasted_iota(jnp.int32, (slots, 1), 0) < live_ref[0]
    for c in range(channels):
        rows = jnp.where(keep, mult_ref[c].astype(F32).T, 0.0).astype(BF16)
        rows = jnp.concatenate([rows, jnp.zeros((slots, KPAD - points), BF16)], axis=1)
        out_ref[:, c * KPAD : (c + 1) * KPAD] = rows


def local_rows(live, multipoles):
    channels, points, slots = multipoles.shape
    return pl.pallas_call(
        local_kernel,
        in_specs=[
            pl.BlockSpec(memory_space=pltpu.SMEM),
            pl.BlockSpec(memory_space=pltpu.VMEM),
        ],
        out_specs=pl.BlockSpec(memory_space=pltpu.VMEM),
        out_shape=jax.ShapeDtypeStruct((slots, channels * KPAD), BF16),
        compiler_params=pltpu.CompilerParams(vmem_limit_bytes=40 * 2**20),
    )(live, multipoles)


def ops_kernel(t_ref, out_ref):
    points = t_ref.shape[1]
    out_ref[...] = jnp.zeros_like(out_ref)
    for k in range(t_ref.shape[0]):
        out_ref[k, :points, :points] = t_ref[k].astype(F32).T.astype(BF16)


def padded_ops(ops, count):
    rel, points, _ = ops.shape
    return pl.pallas_call(
        ops_kernel,
        grid=(rel // count,),
        in_specs=[pl.BlockSpec((count, points, points), lambda i: (i, 0, 0))],
        out_specs=pl.BlockSpec((count, KPAD, KPAD), lambda i: (i, 0, 0)),
        out_shape=jax.ShapeDtypeStruct((rel, KPAD, KPAD), BF16),
        compiler_params=pltpu.CompilerParams(vmem_limit_bytes=16 * 2**20),
    )(ops)


def m2l_kernel(
    vl_ref, live_ref, arr_hbm, loc_hbm, t_hbm, out_ref, buf, acc, arr_ref, loc_ref, t_ref, loc_sem, arr_sem, t_sem, *, depth, batch
):
    slots = loc_ref.shape[0]
    ghosts = arr_ref.shape[0]
    parts = arr_sem.shape[0]
    span = ghosts // parts
    channels, points, _ = out_ref.shape
    chunks = KPAD // LANES
    groups = t_hbm.shape[0] // depth
    laps = groups // 2
    first = (slots + ghosts + 4) * BOX

    def start(p):
        return first + p * slots * BOX

    def gather(r, p, t0, t1):
        base = r * slots
        for tb in range(t0, t1, batch):
            held = []
            for t in range(tb, tb + batch):
                i = vl_ref[base + t]
                held.append((start(p) + t * BOX, buf[pl.ds(i, 8), :], buf[pl.ds(i + 8, BOX - 8), :]))
            for to, head, tail in held:
                buf[pl.ds(to, 8), :] = head
                buf[pl.ds(to + 8, BOX - 8), :] = tail

    def ops_copy(lap):
        place = lax.rem(lap, 2)
        return pltpu.make_async_copy(t_hbm.at[pl.ds(lap * 2 * depth, 2 * depth)], t_ref.at[place], t_sem.at[place])

    def part_copy(k):
        rows = pl.ds(k * span, span)
        return pltpu.make_async_copy(arr_hbm.at[rows], arr_ref.at[rows], arr_sem.at[k])

    def fill(ref, low, count, at):
        def one(b, carry):
            rows = ref[pl.ds(pl.multiple_of(low + b * 16, 16), 16), :].astype(F32)
            for q in range(BOX):
                buf[pl.ds((at + b * 16) * BOX + q, 16, stride=BOX), :] = rows[:, q * LANES : (q + 1) * LANES]
            return carry

        lax.fori_loop(0, count // 16, one, 0, unroll=2)

    loc_copy = pltpu.make_async_copy(loc_hbm, loc_ref, loc_sem)
    loc_copy.start()
    for k in range(parts):
        part_copy(k).start()
    ops_copy(0).start()
    loc_copy.wait()
    fill(loc_ref, 0, slots, 0)
    for k in range(parts):
        part_copy(k).wait()
        fill(arr_ref, k * span, span, slots + k * span)
    buf[pl.ds((slots + ghosts) * BOX, 16), :] = jnp.zeros((16, LANES), F32)
    acc[...] = jnp.zeros_like(acc)
    for p in range(depth):
        gather(p, p, 0, slots)

    def group(s, slot, place):
        later = jnp.minimum(s + 1, groups - 1)
        total = depth * slots
        cuts = [total * c // channels // batch * batch for c in range(channels + 1)]
        for c in range(channels):
            for p in range(depth):
                lo, hi = max(cuts[c] - p * slots, 0), min(cuts[c + 1] - p * slots, slots)
                if lo < hi:
                    gather(later * depth + p, (1 - slot) * depth + p, lo, hi)
            x = jnp.concatenate(
                [
                    buf[pl.ds(start(slot * depth + p) + c * chunks + q, slots, stride=BOX), :].astype(BF16)
                    for p in range(depth)
                    for q in range(chunks)
                ],
                axis=1,
            )
            w = t_ref[place, slot * depth : (slot + 1) * depth].reshape(depth * KPAD, KPAD)
            acc[c] += jnp.dot(x, w, preferred_element_type=F32)

    def lap(s, carry):
        place = lax.rem(s, 2)
        ops_copy(s).wait()

        @pl.when(s + 1 < laps)
        def _():
            ops_copy(s + 1).start()

        group(2 * s, 0, place)
        group(2 * s + 1, 1, place)
        return carry

    lax.fori_loop(0, laps, lap, 0)
    keep = lax.broadcasted_iota(jnp.int32, (1, slots), 1) < live_ref[0]
    for c in range(channels):
        out_ref[c] = jnp.where(keep, acc[c].T[:points], 0.0)


def m2l(cols, live, arrived, local, ops, channels, points):
    ghosts = arrived.shape[0]
    slots = local.shape[0]
    depth = 2
    smem = pl.BlockSpec(memory_space=pltpu.SMEM)
    hbm = pl.BlockSpec(memory_space=pl.ANY)
    return pl.pallas_call(
        functools.partial(m2l_kernel, depth=depth, batch=16),
        in_specs=[smem, smem, hbm, hbm, hbm],
        out_specs=pl.BlockSpec(memory_space=pltpu.VMEM),
        scratch_shapes=[
            pltpu.VMEM(((slots + ghosts + 4 + 2 * depth * slots) * BOX, LANES), F32),
            pltpu.VMEM((channels, slots, KPAD), F32),
            pltpu.VMEM(arrived.shape, BF16),
            pltpu.VMEM(local.shape, BF16),
            pltpu.VMEM((2, 2 * depth, KPAD, KPAD), BF16),
            pltpu.SemaphoreType.DMA,
            pltpu.SemaphoreType.DMA((4,)),
            pltpu.SemaphoreType.DMA((2,)),
        ],
        out_shape=jax.ShapeDtypeStruct((channels, points, slots), F32),
        compiler_params=pltpu.CompilerParams(vmem_limit_bytes=56 * 2**20),
    )(cols, live, arrived, local, ops)


def shifted(cells, step):
    count = lax.axis_size("morton")
    if step > 0:
        pairs = [(i, i + 1) for i in range(count - 1)]
    else:
        pairs = [(i + 1, i) for i in range(count - 1)]
    return lax.ppermute(cells, "morton", pairs)


def body(multipoles, upward_ops, transfer_ops, live_counts, seam_joins, send_slots, vlist_cols):
    channels, points, slot_total = multipoles.shape
    group_total = slot_total // 8
    dev_count = lax.axis_size("morton")
    ghosts = send_slots.shape[1]
    width = channels * KPAD
    outgoing = pack(multipoles, send_slots)
    outgoing, multipoles, transfer_ops = lax.optimization_barrier((outgoing, multipoles, transfer_ops))
    arrived = lax.all_to_all(
        outgoing.reshape(dev_count, ghosts // dev_count, width), "morton", 0, 0, tiled=True
    ).reshape(ghosts, width)

    local = local_rows(live_counts, multipoles)
    ops = padded_ops(transfer_ops, 2)
    cols = (vlist_cols.T * BOX).reshape(-1)

    slot_ids = jnp.arange(slot_total, dtype=jnp.int32)
    keep = (slot_ids < live_counts[0])[None, None, :]
    masked = jnp.where(keep, multipoles, jnp.zeros_like(multipoles))
    children = masked.reshape(channels, points, group_total, 8)
    partial_value = jnp.einsum("oij,cjgo->cig", upward_ops, children, preferred_element_type=F32)
    last_group = (live_counts[0] - 1) // 8
    last_part = lax.dynamic_slice_in_dim(partial_value, last_group, 1, 2)[:, :, 0]
    from_left = shifted(last_part, 1)
    from_right = shifted(partial_value[:, :, 0], -1)
    group_ids = jnp.arange(group_total, dtype=jnp.int32)
    joins = seam_joins[0].astype(F32)
    parent_mult = partial_value + jnp.where(
        (group_ids == 0)[None, None, :], (joins[0] * from_left)[:, :, None], F32(0.0)
    )
    parent_mult = parent_mult + jnp.where(
        (group_ids == last_group)[None, None, :], (joins[1] * from_right)[:, :, None], F32(0.0)
    )
    local_check = m2l(cols, live_counts, arrived, local, ops, channels, points)
    return (local_check, parent_mult)


def solution(mesh):
    placed = (
        P(None, None, "morton"),
        P(),
        P(),
        P("morton"),
        P("morton", None),
        P("morton", None),
        P("morton", None),
    )
    return jax.shard_map(
        body,
        mesh=mesh,
        in_specs=placed,
        out_specs=(P(None, None, "morton"), P(None, None, "morton")),
        check_vma=False,
    )
```

```python
import functools

import jax
import jax.numpy as jnp
from jax import lax
from jax.experimental import pallas as pl
from jax.experimental.pallas import tpu as pltpu
from jax.sharding import PartitionSpec as P

BOX = 12
LANES = 128
KPAD = 512
BF16 = jnp.bfloat16
F32 = jnp.float32


def pack_kernel(mult_ref, slots_ref, out_ref):
    channels, points, send_slots = mult_ref.shape
    ghosts = slots_ref.shape[1]
    box_ids = lax.broadcasted_iota(jnp.int32, (send_slots, ghosts), 0)
    onehot = jnp.where(box_ids == slots_ref[...], 1.0, 0.0).astype(BF16)
    for c in range(channels):
        rows = lax.dot_general(
            onehot, mult_ref[c], (((0,), (1,)), ((), ())), preferred_element_type=F32
        ).astype(BF16)
        rows = jnp.concatenate([rows, jnp.zeros((ghosts, KPAD - points), BF16)], axis=1)
        out_ref[:, c * KPAD : (c + 1) * KPAD] = rows


def pack(multipoles, send_slots):
    channels, points, slots = multipoles.shape
    ghosts = send_slots.shape[1]
    half = slots // 2
    block = 256
    return pl.pallas_call(
        pack_kernel,
        grid=(ghosts // block,),
        in_specs=[
            pl.BlockSpec((channels, points, half), lambda i: (0, 0, 0)),
            pl.BlockSpec((1, block), lambda i: (0, i)),
        ],
        out_specs=pl.BlockSpec((block, channels * KPAD), lambda i: (i, 0)),
        out_shape=jax.ShapeDtypeStruct((ghosts, channels * KPAD), BF16),
        compiler_params=pltpu.CompilerParams(vmem_limit_bytes=60 * 2**20),
    )(multipoles, send_slots)


def local_kernel(live_ref, mult_ref, out_ref):
    channels, points, slots = mult_ref.shape
    keep = lax.broadcasted_iota(jnp.int32, (slots, 1), 0) < live_ref[0]
    for c in range(channels):
        rows = jnp.where(keep, mult_ref[c].astype(F32).T, 0.0).astype(BF16)
        rows = jnp.concatenate([rows, jnp.zeros((slots, KPAD - points), BF16)], axis=1)
        out_ref[:, c * KPAD : (c + 1) * KPAD] = rows


def local_rows(live, multipoles):
    channels, points, slots = multipoles.shape
    return pl.pallas_call(
        local_kernel,
        in_specs=[
            pl.BlockSpec(memory_space=pltpu.SMEM),
            pl.BlockSpec(memory_space=pltpu.VMEM),
        ],
        out_specs=pl.BlockSpec(memory_space=pltpu.VMEM),
        out_shape=jax.ShapeDtypeStruct((slots, channels * KPAD), BF16),
        compiler_params=pltpu.CompilerParams(vmem_limit_bytes=40 * 2**20),
    )(live, multipoles)


def ops_kernel(t_ref, out_ref):
    points = t_ref.shape[1]
    out_ref[...] = jnp.zeros_like(out_ref)
    for k in range(t_ref.shape[0]):
        out_ref[k, :points, :points] = t_ref[k].astype(F32).T.astype(BF16)


def padded_ops(ops, count):
    rel, points, _ = ops.shape
    return pl.pallas_call(
        ops_kernel,
        grid=(rel // count,),
        in_specs=[pl.BlockSpec((count, points, points), lambda i: (i, 0, 0))],
        out_specs=pl.BlockSpec((count, KPAD, KPAD), lambda i: (i, 0, 0)),
        out_shape=jax.ShapeDtypeStruct((rel, KPAD, KPAD), BF16),
        compiler_params=pltpu.CompilerParams(vmem_limit_bytes=16 * 2**20),
    )(ops)


def m2l_kernel(
    vl_ref, live_ref, arr_hbm, loc_hbm, t_hbm, out_hbm, buf, acc, arr_ref, loc_ref, t_ref, stage, loc_sem, arr_sem, t_sem, out_sem, *, depth, batch
):
    slots = loc_ref.shape[0]
    ghosts = arr_ref.shape[0]
    parts = arr_sem.shape[0]
    span = ghosts // parts
    channels, points, _ = stage.shape
    chunks = KPAD // LANES
    groups = t_hbm.shape[0] // depth
    laps = groups // 2
    first = (slots + ghosts + 4) * BOX

    def start(p):
        return first + p * slots * BOX

    def gather(r, p, t0, t1):
        base = r * slots
        for tb in range(t0, t1, batch):
            held = []
            for t in range(tb, tb + batch):
                i = vl_ref[base + t]
                held.append((start(p) + t * BOX, buf[pl.ds(i, 8), :], buf[pl.ds(i + 8, BOX - 8), :]))
            for to, head, tail in held:
                buf[pl.ds(to, 8), :] = head
                buf[pl.ds(to + 8, BOX - 8), :] = tail

    def ops_copy(lap):
        place = lax.rem(lap, 2)
        return pltpu.make_async_copy(t_hbm.at[pl.ds(lap * 2 * depth, 2 * depth)], t_ref.at[place], t_sem.at[place])

    def part_copy(k):
        rows = pl.ds(k * span, span)
        return pltpu.make_async_copy(arr_hbm.at[rows], arr_ref.at[rows], arr_sem.at[k])

    def fill(ref, low, count, at):
        def one(b, carry):
            rows = ref[pl.ds(pl.multiple_of(low + b * 16, 16), 16), :].astype(F32)
            for q in range(BOX):
                buf[pl.ds((at + b * 16) * BOX + q, 16, stride=BOX), :] = rows[:, q * LANES : (q + 1) * LANES]
            return carry

        lax.fori_loop(0, count // 16, one, 0, unroll=2)

    loc_copy = pltpu.make_async_copy(loc_hbm, loc_ref, loc_sem)
    loc_copy.start()
    for k in range(parts):
        part_copy(k).start()
    ops_copy(0).start()
    acc[...] = jnp.zeros_like(acc)
    loc_copy.wait()
    fill(loc_ref, 0, slots, 0)
    for k in range(parts):
        part_copy(k).wait()
        fill(arr_ref, k * span, span, slots + k * span)
    buf[pl.ds((slots + ghosts) * BOX, 16), :] = jnp.zeros((16, LANES), F32)
    for p in range(depth):
        gather(p, p, 0, slots)

    def group(s, slot, place):
        later = jnp.minimum(s + 1, groups - 1)
        total = depth * slots
        cuts = [total * c // channels // batch * batch for c in range(channels + 1)]
        for c in range(channels):
            for p in range(depth):
                lo, hi = max(cuts[c] - p * slots, 0), min(cuts[c + 1] - p * slots, slots)
                if lo < hi:
                    gather(later * depth + p, (1 - slot) * depth + p, lo, hi)
            x = jnp.concatenate(
                [
                    buf[pl.ds(start(slot * depth + p) + c * chunks + q, slots, stride=BOX), :].astype(BF16)
                    for p in range(depth)
                    for q in range(chunks)
                ],
                axis=1,
            )
            w = t_ref[place, slot * depth : (slot + 1) * depth].reshape(depth * KPAD, KPAD)
            acc[c] += jnp.dot(x, w, preferred_element_type=F32)

    def lap(s, carry):
        place = lax.rem(s, 2)
        ops_copy(s).wait()

        @pl.when(s + 1 < laps)
        def _():
            ops_copy(s + 1).start()

        group(2 * s, 0, place)
        group(2 * s + 1, 1, place)
        return carry

    lax.fori_loop(0, laps, lap, 0)
    keep = lax.broadcasted_iota(jnp.int32, (1, slots), 1) < live_ref[0]
    out_copies = []
    for c in range(channels):
        stage[c] = jnp.where(keep, acc[c].T[:points], 0.0)
        out_copies.append(pltpu.make_async_copy(stage.at[c], out_hbm.at[c], out_sem.at[c]))
        out_copies[c].start()
    for copy in out_copies:
        copy.wait()


def m2l(cols, live, arrived, local, ops, channels, points):
    ghosts = arrived.shape[0]
    slots = local.shape[0]
    depth = 2
    smem = pl.BlockSpec(memory_space=pltpu.SMEM)
    hbm = pl.BlockSpec(memory_space=pl.ANY)
    return pl.pallas_call(
        functools.partial(m2l_kernel, depth=depth, batch=8),
        in_specs=[smem, smem, hbm, hbm, hbm],
        out_specs=hbm,
        scratch_shapes=[
            pltpu.VMEM(((slots + ghosts + 4 + 2 * depth * slots) * BOX, LANES), F32),
            pltpu.VMEM((channels, slots, KPAD), F32),
            pltpu.VMEM(arrived.shape, BF16),
            pltpu.VMEM(local.shape, BF16),
            pltpu.VMEM((2, 2 * depth, KPAD, KPAD), BF16),
            pltpu.VMEM((channels, points, slots), F32),
            pltpu.SemaphoreType.DMA,
            pltpu.SemaphoreType.DMA((4,)),
            pltpu.SemaphoreType.DMA((2,)),
            pltpu.SemaphoreType.DMA((channels,)),
        ],
        out_shape=jax.ShapeDtypeStruct((channels, points, slots), F32),
        compiler_params=pltpu.CompilerParams(vmem_limit_bytes=56 * 2**20),
    )(cols, live, arrived, local, ops)


def shifted(cells, step):
    count = lax.axis_size("morton")
    if step > 0:
        pairs = [(i, i + 1) for i in range(count - 1)]
    else:
        pairs = [(i + 1, i) for i in range(count - 1)]
    return lax.ppermute(cells, "morton", pairs)


def body(multipoles, upward_ops, transfer_ops, live_counts, seam_joins, send_slots, vlist_cols):
    channels, points, slot_total = multipoles.shape
    group_total = slot_total // 8
    dev_count = lax.axis_size("morton")
    ghosts = send_slots.shape[1]
    width = channels * KPAD
    outgoing = pack(multipoles, send_slots)
    outgoing, multipoles, transfer_ops = lax.optimization_barrier((outgoing, multipoles, transfer_ops))
    arrived = lax.all_to_all(
        outgoing.reshape(dev_count, ghosts // dev_count, width), "morton", 0, 0, tiled=True
    ).reshape(ghosts, width)

    local = local_rows(live_counts, multipoles)
    ops = padded_ops(transfer_ops, 2)
    cols = (vlist_cols.T * BOX).reshape(-1)

    slot_ids = jnp.arange(slot_total, dtype=jnp.int32)
    keep = (slot_ids < live_counts[0])[None, None, :]
    masked = jnp.where(keep, multipoles, jnp.zeros_like(multipoles))
    children = masked.reshape(channels, points, group_total, 8)
    partial_value = jnp.einsum("oij,cjgo->cig", upward_ops, children, preferred_element_type=F32)
    last_group = (live_counts[0] - 1) // 8
    last_part = lax.dynamic_slice_in_dim(partial_value, last_group, 1, 2)[:, :, 0]
    from_left = shifted(last_part, 1)
    from_right = shifted(partial_value[:, :, 0], -1)
    group_ids = jnp.arange(group_total, dtype=jnp.int32)
    joins = seam_joins[0].astype(F32)
    parent_mult = partial_value + jnp.where(
        (group_ids == 0)[None, None, :], (joins[0] * from_left)[:, :, None], F32(0.0)
    )
    parent_mult = parent_mult + jnp.where(
        (group_ids == last_group)[None, None, :], (joins[1] * from_right)[:, :, None], F32(0.0)
    )
    local_check = m2l(cols, live_counts, arrived, local, ops, channels, points)
    return (local_check, parent_mult)


def solution(mesh):
    placed = (
        P(None, None, "morton"),
        P(),
        P(),
        P("morton"),
        P("morton", None),
        P("morton", None),
        P("morton", None),
    )
    return jax.shard_map(
        body,
        mesh=mesh,
        in_specs=placed,
        out_specs=(P(None, None, "morton"), P(None, None, "morton")),
        check_vma=False,
    )
```

```python
import functools

import jax
import jax.numpy as jnp
from jax import lax
from jax.experimental import pallas as pl
from jax.experimental.pallas import tpu as pltpu
from jax.sharding import PartitionSpec as P

BOX = 12
LANES = 128
KPAD = 512
BF16 = jnp.bfloat16
F32 = jnp.float32


def pack_kernel(mult_ref, slots_ref, out_hbm, rows_ref, sem):
    channels, points, send_slots = mult_ref.shape
    parts = sem.shape[0]
    span = rows_ref.shape[0] // parts
    box_ids = lax.broadcasted_iota(jnp.int32, (send_slots, span), 0)
    copies = []
    for k in range(parts):
        at = slice(k * span, (k + 1) * span)
        onehot = jnp.where(box_ids == slots_ref[:, at], 1.0, 0.0).astype(BF16)
        for c in range(channels):
            rows = lax.dot_general(
                onehot, mult_ref[c], (((0,), (1,)), ((), ())), preferred_element_type=F32
            ).astype(BF16)
            rows = jnp.concatenate([rows, jnp.zeros((span, KPAD - points), BF16)], axis=1)
            rows_ref[at, c * KPAD : (c + 1) * KPAD] = rows
        copies.append(pltpu.make_async_copy(rows_ref.at[at], out_hbm.at[at], sem.at[k]))
        copies[k].start()
    for copy in copies:
        copy.wait()


def pack(multipoles, send_slots):
    channels, points, slots = multipoles.shape
    ghosts = send_slots.shape[1]
    half = slots // 2
    return pl.pallas_call(
        pack_kernel,
        grid=(1,),
        in_specs=[
            pl.BlockSpec((channels, points, half), lambda i: (0, 0, 0)),
            pl.BlockSpec((1, ghosts), lambda i: (0, 0)),
        ],
        out_specs=pl.BlockSpec(memory_space=pl.ANY),
        out_shape=jax.ShapeDtypeStruct((ghosts, channels * KPAD), BF16),
        scratch_shapes=[
            pltpu.VMEM((ghosts, channels * KPAD), BF16),
            pltpu.SemaphoreType.DMA((ghosts // 256,)),
        ],
        compiler_params=pltpu.CompilerParams(vmem_limit_bytes=60 * 2**20),
    )(multipoles, send_slots)


def local_kernel(live_ref, mult_ref, out_ref):
    channels, points, slots = mult_ref.shape
    keep = lax.broadcasted_iota(jnp.int32, (slots, 1), 0) < live_ref[0]
    for c in range(channels):
        rows = jnp.where(keep, mult_ref[c].astype(F32).T, 0.0).astype(BF16)
        rows = jnp.concatenate([rows, jnp.zeros((slots, KPAD - points), BF16)], axis=1)
        out_ref[:, c * KPAD : (c + 1) * KPAD] = rows


def local_rows(live, multipoles):
    channels, points, slots = multipoles.shape
    return pl.pallas_call(
        local_kernel,
        in_specs=[
            pl.BlockSpec(memory_space=pltpu.SMEM),
            pl.BlockSpec(memory_space=pltpu.VMEM),
        ],
        out_specs=pl.BlockSpec(memory_space=pltpu.VMEM),
        out_shape=jax.ShapeDtypeStruct((slots, channels * KPAD), BF16),
        compiler_params=pltpu.CompilerParams(vmem_limit_bytes=40 * 2**20),
    )(live, multipoles)


def ops_kernel(t_ref, out_ref):
    points = t_ref.shape[1]
    out_ref[...] = jnp.zeros_like(out_ref)
    for k in range(t_ref.shape[0]):
        out_ref[k, :points, :points] = t_ref[k].astype(F32).T.astype(BF16)


def padded_ops(ops, count):
    rel, points, _ = ops.shape
    return pl.pallas_call(
        ops_kernel,
        grid=(rel // count,),
        in_specs=[pl.BlockSpec((count, points, points), lambda i: (i, 0, 0))],
        out_specs=pl.BlockSpec((count, KPAD, KPAD), lambda i: (i, 0, 0)),
        out_shape=jax.ShapeDtypeStruct((rel, KPAD, KPAD), BF16),
        compiler_params=pltpu.CompilerParams(vmem_limit_bytes=16 * 2**20),
    )(ops)


def m2l_kernel(
    vl_ref, live_ref, arr_hbm, loc_hbm, t_hbm, out_hbm, buf, acc, arr_ref, loc_ref, t_ref, stage, loc_sem, arr_sem, t_sem, out_sem, *, depth, batch
):
    slots = loc_ref.shape[0]
    ghosts = arr_ref.shape[0]
    parts = arr_sem.shape[0]
    span = ghosts // parts
    channels, points, _ = stage.shape
    chunks = KPAD // LANES
    groups = t_hbm.shape[0] // depth
    laps = groups // 2
    first = (slots + ghosts + 4) * BOX

    def start(p):
        return first + p * slots * BOX

    def gather(r, p, t0, t1):
        base = r * slots
        for tb in range(t0, t1, batch):
            held = []
            for t in range(tb, tb + batch):
                i = vl_ref[base + t]
                held.append((start(p) + t * BOX, buf[pl.ds(i, 8), :], buf[pl.ds(i + 8, BOX - 8), :]))
            for to, head, tail in held:
                buf[pl.ds(to, 8), :] = head
                buf[pl.ds(to + 8, BOX - 8), :] = tail

    def ops_copy(lap):
        place = lax.rem(lap, 2)
        return pltpu.make_async_copy(t_hbm.at[pl.ds(lap * 2 * depth, 2 * depth)], t_ref.at[place], t_sem.at[place])

    def part_copy(k):
        rows = pl.ds(k * span, span)
        return pltpu.make_async_copy(arr_hbm.at[rows], arr_ref.at[rows], arr_sem.at[k])

    def fill(ref, low, count, at):
        def one(b, carry):
            rows = ref[pl.ds(pl.multiple_of(low + b * 16, 16), 16), :].astype(F32)
            for q in range(BOX):
                buf[pl.ds((at + b * 16) * BOX + q, 16, stride=BOX), :] = rows[:, q * LANES : (q + 1) * LANES]
            return carry

        lax.fori_loop(0, count // 16, one, 0, unroll=2)

    loc_copy = pltpu.make_async_copy(loc_hbm, loc_ref, loc_sem)
    loc_copy.start()
    for k in range(parts):
        part_copy(k).start()
    ops_copy(0).start()
    acc[...] = jnp.zeros_like(acc)
    loc_copy.wait()
    fill(loc_ref, 0, slots, 0)
    for k in range(parts):
        part_copy(k).wait()
        fill(arr_ref, k * span, span, slots + k * span)
    buf[pl.ds((slots + ghosts) * BOX, 16), :] = jnp.zeros((16, LANES), F32)
    for p in range(depth):
        gather(p, p, 0, slots)

    def group(s, slot, place):
        later = jnp.minimum(s + 1, groups - 1)
        total = depth * slots
        cuts = [total * c // channels // batch * batch for c in range(channels + 1)]
        def fetch(c):
            for p in range(depth):
                lo, hi = max(cuts[c] - p * slots, 0), min(cuts[c + 1] - p * slots, slots)
                if lo < hi:
                    gather(later * depth + p, (1 - slot) * depth + p, lo, hi)

        def multiply(c):
            x = jnp.concatenate(
                [
                    buf[pl.ds(start(slot * depth + p) + c * chunks + q, slots, stride=BOX), :].astype(BF16)
                    for p in range(depth)
                    for q in range(chunks)
                ],
                axis=1,
            )
            w = t_ref[place, slot * depth : (slot + 1) * depth].reshape(depth * KPAD, KPAD)
            acc[c] += jnp.dot(x, w, preferred_element_type=F32)

        for c in range(channels):
            fetch(c)
            multiply(c)

    def lap(s, carry):
        place = lax.rem(s, 2)
        ops_copy(s).wait()

        @pl.when(s + 1 < laps)
        def _():
            ops_copy(s + 1).start()

        group(2 * s, 0, place)
        group(2 * s + 1, 1, place)
        return carry

    lax.fori_loop(0, laps, lap, 0)
    keep = lax.broadcasted_iota(jnp.int32, (1, slots), 1) < live_ref[0]
    out_copies = []
    for c in range(channels):
        stage[c] = jnp.where(keep, acc[c].T[:points], 0.0)
        out_copies.append(pltpu.make_async_copy(stage.at[c], out_hbm.at[c], out_sem.at[c]))
        out_copies[c].start()
    for copy in out_copies:
        copy.wait()


def m2l(cols, live, arrived, local, ops, channels, points):
    ghosts = arrived.shape[0]
    slots = local.shape[0]
    depth = 2
    smem = pl.BlockSpec(memory_space=pltpu.SMEM)
    hbm = pl.BlockSpec(memory_space=pl.ANY)
    return pl.pallas_call(
        functools.partial(m2l_kernel, depth=depth, batch=8),
        in_specs=[smem, smem, hbm, hbm, hbm],
        out_specs=hbm,
        scratch_shapes=[
            pltpu.VMEM(((slots + ghosts + 4 + 2 * depth * slots) * BOX, LANES), F32),
            pltpu.VMEM((channels, slots, KPAD), F32),
            pltpu.VMEM(arrived.shape, BF16),
            pltpu.VMEM(local.shape, BF16),
            pltpu.VMEM((2, 2 * depth, KPAD, KPAD), BF16),
            pltpu.VMEM((channels, points, slots), F32),
            pltpu.SemaphoreType.DMA,
            pltpu.SemaphoreType.DMA((4,)),
            pltpu.SemaphoreType.DMA((2,)),
            pltpu.SemaphoreType.DMA((channels,)),
        ],
        out_shape=jax.ShapeDtypeStruct((channels, points, slots), F32),
        compiler_params=pltpu.CompilerParams(vmem_limit_bytes=56 * 2**20),
    )(cols, live, arrived, local, ops)


def shifted(cells, step):
    count = lax.axis_size("morton")
    if step > 0:
        pairs = [(i, i + 1) for i in range(count - 1)]
    else:
        pairs = [(i + 1, i) for i in range(count - 1)]
    return lax.ppermute(cells, "morton", pairs)


def body(multipoles, upward_ops, transfer_ops, live_counts, seam_joins, send_slots, vlist_cols):
    channels, points, slot_total = multipoles.shape
    group_total = slot_total // 8
    dev_count = lax.axis_size("morton")
    ghosts = send_slots.shape[1]
    width = channels * KPAD
    outgoing = pack(multipoles, send_slots)
    outgoing, multipoles, transfer_ops = lax.optimization_barrier((outgoing, multipoles, transfer_ops))
    arrived = lax.all_to_all(
        outgoing.reshape(dev_count, ghosts // dev_count, width), "morton", 0, 0, tiled=True
    ).reshape(ghosts, width)

    local = local_rows(live_counts, multipoles)
    ops = padded_ops(transfer_ops, 2)
    cols = (vlist_cols.T * BOX).reshape(-1)

    slot_ids = jnp.arange(slot_total, dtype=jnp.int32)
    keep = (slot_ids < live_counts[0])[None, None, :]
    masked = jnp.where(keep, multipoles, jnp.zeros_like(multipoles))
    children = masked.reshape(channels, points, group_total, 8)
    partial_value = jnp.einsum("oij,cjgo->cig", upward_ops, children, preferred_element_type=F32)
    last_group = (live_counts[0] - 1) // 8
    last_part = lax.dynamic_slice_in_dim(partial_value, last_group, 1, 2)[:, :, 0]
    from_left = shifted(last_part, 1)
    from_right = shifted(partial_value[:, :, 0], -1)
    group_ids = jnp.arange(group_total, dtype=jnp.int32)
    joins = seam_joins[0].astype(F32)
    parent_mult = partial_value + jnp.where(
        (group_ids == 0)[None, None, :], (joins[0] * from_left)[:, :, None], F32(0.0)
    )
    parent_mult = parent_mult + jnp.where(
        (group_ids == last_group)[None, None, :], (joins[1] * from_right)[:, :, None], F32(0.0)
    )
    local_check = m2l(cols, live_counts, arrived, local, ops, channels, points)
    return (local_check, parent_mult)


def solution(mesh):
    placed = (
        P(None, None, "morton"),
        P(),
        P(),
        P("morton"),
        P("morton", None),
        P("morton", None),
        P("morton", None),
    )
    return jax.shard_map(
        body,
        mesh=mesh,
        in_specs=placed,
        out_specs=(P(None, None, "morton"), P(None, None, "morton")),
        check_vma=False,
    )
```

```python
import functools

import jax
import jax.numpy as jnp
from jax import lax
from jax.experimental import pallas as pl
from jax.experimental.pallas import tpu as pltpu
from jax.sharding import PartitionSpec as P

BOX = 12
LANES = 128
KPAD = 512
BF16 = jnp.bfloat16
F32 = jnp.float32


def pack_kernel(mult_ref, slots_ref, out_hbm, rows_ref, sem):
    channels, points, send_slots = mult_ref.shape
    parts = sem.shape[0]
    span = rows_ref.shape[0] // parts
    box_ids = lax.broadcasted_iota(jnp.int32, (send_slots, span), 0)
    copies = []
    for k in range(parts):
        at = slice(k * span, (k + 1) * span)
        onehot = jnp.where(box_ids == slots_ref[:, at], 1.0, 0.0).astype(BF16)
        for c in range(channels):
            rows = lax.dot_general(
                onehot, mult_ref[c], (((0,), (1,)), ((), ())), preferred_element_type=F32
            ).astype(BF16)
            rows = jnp.concatenate([rows, jnp.zeros((span, KPAD - points), BF16)], axis=1)
            rows_ref[at, c * KPAD : (c + 1) * KPAD] = rows
        copies.append(pltpu.make_async_copy(rows_ref.at[at], out_hbm.at[at], sem.at[k]))
        copies[k].start()
    for copy in copies:
        copy.wait()


def pack(multipoles, send_slots):
    channels, points, slots = multipoles.shape
    ghosts = send_slots.shape[1]
    half = slots // 2
    return pl.pallas_call(
        pack_kernel,
        grid=(1,),
        in_specs=[
            pl.BlockSpec((channels, points, half), lambda i: (0, 0, 0)),
            pl.BlockSpec((1, ghosts), lambda i: (0, 0)),
        ],
        out_specs=pl.BlockSpec(memory_space=pl.ANY),
        out_shape=jax.ShapeDtypeStruct((ghosts, channels * KPAD), BF16),
        scratch_shapes=[
            pltpu.VMEM((ghosts, channels * KPAD), BF16),
            pltpu.SemaphoreType.DMA((ghosts // 256,)),
        ],
        compiler_params=pltpu.CompilerParams(vmem_limit_bytes=60 * 2**20),
    )(multipoles, send_slots)


def local_kernel(live_ref, mult_ref, out_ref):
    channels, points, slots = mult_ref.shape
    keep = lax.broadcasted_iota(jnp.int32, (slots, 1), 0) < live_ref[0]
    for c in range(channels):
        rows = jnp.where(keep, mult_ref[c].astype(F32).T, 0.0).astype(BF16)
        rows = jnp.concatenate([rows, jnp.zeros((slots, KPAD - points), BF16)], axis=1)
        out_ref[:, c * KPAD : (c + 1) * KPAD] = rows


def local_rows(live, multipoles):
    channels, points, slots = multipoles.shape
    return pl.pallas_call(
        local_kernel,
        in_specs=[
            pl.BlockSpec(memory_space=pltpu.SMEM),
            pl.BlockSpec(memory_space=pltpu.VMEM),
        ],
        out_specs=pl.BlockSpec(memory_space=pltpu.VMEM),
        out_shape=jax.ShapeDtypeStruct((slots, channels * KPAD), BF16),
        compiler_params=pltpu.CompilerParams(vmem_limit_bytes=40 * 2**20),
    )(live, multipoles)


def ops_kernel(t_ref, out_ref):
    points = t_ref.shape[1]
    out_ref[...] = jnp.zeros_like(out_ref)
    for k in range(t_ref.shape[0]):
        out_ref[k, :points, :points] = t_ref[k].astype(F32).T.astype(BF16)


def padded_ops(ops, count):
    rel, points, _ = ops.shape
    return pl.pallas_call(
        ops_kernel,
        grid=(rel // count,),
        in_specs=[pl.BlockSpec((count, points, points), lambda i: (i, 0, 0))],
        out_specs=pl.BlockSpec((count, KPAD, KPAD), lambda i: (i, 0, 0)),
        out_shape=jax.ShapeDtypeStruct((rel, KPAD, KPAD), BF16),
        compiler_params=pltpu.CompilerParams(vmem_limit_bytes=16 * 2**20),
    )(ops)


def m2l_kernel(
    vl_ref, live_ref, arr_hbm, loc_hbm, t_hbm, out_hbm, buf, acc, arr_ref, loc_ref, t_ref, stage, loc_sem, arr_sem, t_sem, out_sem, *, depth, batch
):
    slots = loc_ref.shape[0]
    ghosts = arr_ref.shape[0]
    parts = arr_sem.shape[0]
    span = ghosts // parts
    channels, points, _ = stage.shape
    chunks = KPAD // LANES
    groups = t_hbm.shape[0] // depth
    laps = groups // 2
    first = (slots + ghosts + 4) * BOX

    def start(p):
        return first + p * slots * BOX

    def gather(r, p, t0, t1):
        base = r * slots
        for tb in range(t0, t1, batch):
            held = []
            for t in range(tb, tb + batch):
                i = vl_ref[base + t]
                held.append((start(p) + t * BOX, buf[pl.ds(i, 8), :], buf[pl.ds(i + 8, BOX - 8), :]))
            for to, head, tail in held:
                buf[pl.ds(to, 8), :] = head
                buf[pl.ds(to + 8, BOX - 8), :] = tail

    def ops_copy(lap):
        place = lax.rem(lap, 2)
        return pltpu.make_async_copy(t_hbm.at[pl.ds(lap * 2 * depth, 2 * depth)], t_ref.at[place], t_sem.at[place])

    def part_copy(k):
        rows = pl.ds(k * span, span)
        return pltpu.make_async_copy(arr_hbm.at[rows], arr_ref.at[rows], arr_sem.at[k])

    def fill(ref, low, count, at):
        def one(b, carry):
            rows = ref[pl.ds(pl.multiple_of(low + b * 16, 16), 16), :].astype(F32)
            for q in range(BOX):
                buf[pl.ds((at + b * 16) * BOX + q, 16, stride=BOX), :] = rows[:, q * LANES : (q + 1) * LANES]
            return carry

        lax.fori_loop(0, count // 16, one, 0, unroll=2)

    loc_copy = pltpu.make_async_copy(loc_hbm, loc_ref, loc_sem)
    loc_copy.start()
    for k in range(parts):
        part_copy(k).start()
    ops_copy(0).start()
    acc[...] = jnp.zeros_like(acc)
    loc_copy.wait()
    fill(loc_ref, 0, slots, 0)
    for k in range(parts):
        part_copy(k).wait()
        fill(arr_ref, k * span, span, slots + k * span)
    buf[pl.ds((slots + ghosts) * BOX, 16), :] = jnp.zeros((16, LANES), F32)
    for p in range(depth):
        gather(p, p, 0, slots)

    def group(s, slot, place, last=False):
        later = jnp.minimum(s + 1, groups - 1)
        total = depth * slots
        cuts = [total * c // channels // batch * batch for c in range(channels + 1)]
        def fetch(c):
            for p in range(depth):
                lo, hi = max(cuts[c] - p * slots, 0), min(cuts[c + 1] - p * slots, slots)
                if lo < hi:
                    gather(later * depth + p, (1 - slot) * depth + p, lo, hi)

        def multiply(c):
            x = jnp.concatenate(
                [
                    buf[pl.ds(start(slot * depth + p) + c * chunks + q, slots, stride=BOX), :].astype(BF16)
                    for p in range(depth)
                    for q in range(chunks)
                ],
                axis=1,
            )
            w = t_ref[place, slot * depth : (slot + 1) * depth].reshape(depth * KPAD, KPAD)
            acc[c] += jnp.dot(x, w, preferred_element_type=F32)

        for c in range(channels):
            if not last:
                fetch(c)
            multiply(c)
            if last:
                finish(c)

    keep = lax.broadcasted_iota(jnp.int32, (1, slots), 1) < live_ref[0]

    def out_copy(c):
        return pltpu.make_async_copy(stage.at[c], out_hbm.at[c], out_sem.at[c])

    def finish(c):
        stage[c] = jnp.where(keep, acc[c].T[:points], 0.0)
        out_copy(c).start()

    def lap(s, carry):
        place = lax.rem(s, 2)
        ops_copy(s).wait()
        ops_copy(s + 1).start()
        group(2 * s, 0, place)
        group(2 * s + 1, 1, place)
        return carry

    lax.fori_loop(0, laps - 1, lap, 0)
    end = laps - 1
    ops_copy(end).wait()
    group(2 * end, 0, end % 2)
    group(2 * end + 1, 1, end % 2, last=True)
    for c in range(channels):
        out_copy(c).wait()


def m2l(cols, live, arrived, local, ops, channels, points):
    ghosts = arrived.shape[0]
    slots = local.shape[0]
    depth = 2
    smem = pl.BlockSpec(memory_space=pltpu.SMEM)
    hbm = pl.BlockSpec(memory_space=pl.ANY)
    return pl.pallas_call(
        functools.partial(m2l_kernel, depth=depth, batch=8),
        in_specs=[smem, smem, hbm, hbm, hbm],
        out_specs=hbm,
        scratch_shapes=[
            pltpu.VMEM(((slots + ghosts + 4 + 2 * depth * slots) * BOX, LANES), F32),
            pltpu.VMEM((channels, slots, KPAD), F32),
            pltpu.VMEM(arrived.shape, BF16),
            pltpu.VMEM(local.shape, BF16),
            pltpu.VMEM((2, 2 * depth, KPAD, KPAD), BF16),
            pltpu.VMEM((channels, points, slots), F32),
            pltpu.SemaphoreType.DMA,
            pltpu.SemaphoreType.DMA((4,)),
            pltpu.SemaphoreType.DMA((2,)),
            pltpu.SemaphoreType.DMA((channels,)),
        ],
        out_shape=jax.ShapeDtypeStruct((channels, points, slots), F32),
        compiler_params=pltpu.CompilerParams(vmem_limit_bytes=56 * 2**20),
    )(cols, live, arrived, local, ops)


def shifted(cells, step):
    count = lax.axis_size("morton")
    if step > 0:
        pairs = [(i, i + 1) for i in range(count - 1)]
    else:
        pairs = [(i + 1, i) for i in range(count - 1)]
    return lax.ppermute(cells, "morton", pairs)


def body(multipoles, upward_ops, transfer_ops, live_counts, seam_joins, send_slots, vlist_cols):
    channels, points, slot_total = multipoles.shape
    group_total = slot_total // 8
    dev_count = lax.axis_size("morton")
    ghosts = send_slots.shape[1]
    width = channels * KPAD
    outgoing = pack(multipoles, send_slots)
    outgoing, multipoles, transfer_ops = lax.optimization_barrier((outgoing, multipoles, transfer_ops))
    arrived = lax.all_to_all(
        outgoing.reshape(dev_count, ghosts // dev_count, width), "morton", 0, 0, tiled=True
    ).reshape(ghosts, width)

    local = local_rows(live_counts, multipoles)
    ops = padded_ops(transfer_ops, 2)
    cols = (vlist_cols.T * BOX).reshape(-1)

    slot_ids = jnp.arange(slot_total, dtype=jnp.int32)
    keep = (slot_ids < live_counts[0])[None, None, :]
    masked = jnp.where(keep, multipoles, jnp.zeros_like(multipoles))
    children = masked.reshape(channels, points, group_total, 8)
    partial_value = jnp.einsum("oij,cjgo->cig", upward_ops, children, preferred_element_type=F32)
    last_group = (live_counts[0] - 1) // 8
    last_part = lax.dynamic_slice_in_dim(partial_value, last_group, 1, 2)[:, :, 0]
    from_left = shifted(last_part, 1)
    from_right = shifted(partial_value[:, :, 0], -1)
    group_ids = jnp.arange(group_total, dtype=jnp.int32)
    joins = seam_joins[0].astype(F32)
    parent_mult = partial_value + jnp.where(
        (group_ids == 0)[None, None, :], (joins[0] * from_left)[:, :, None], F32(0.0)
    )
    parent_mult = parent_mult + jnp.where(
        (group_ids == last_group)[None, None, :], (joins[1] * from_right)[:, :, None], F32(0.0)
    )
    local_check = m2l(cols, live_counts, arrived, local, ops, channels, points)
    return (local_check, parent_mult)


def solution(mesh):
    placed = (
        P(None, None, "morton"),
        P(),
        P(),
        P("morton"),
        P("morton", None),
        P("morton", None),
        P("morton", None),
    )
    return jax.shard_map(
        body,
        mesh=mesh,
        in_specs=placed,
        out_specs=(P(None, None, "morton"), P(None, None, "morton")),
        check_vma=False,
    )
```

```python
import functools

import jax
import jax.numpy as jnp
from jax import lax
from jax.experimental import pallas as pl
from jax.experimental.pallas import tpu as pltpu
from jax.sharding import PartitionSpec as P

BOX = 12
LANES = 128
KPAD = 512
BF16 = jnp.bfloat16
F32 = jnp.float32


def pack_kernel(mult_ref, slots_ref, out_hbm, rows_ref, sem):
    channels, points, send_slots = mult_ref.shape
    parts = sem.shape[0]
    span = rows_ref.shape[0] // parts
    box_ids = lax.broadcasted_iota(jnp.int32, (send_slots, span), 0)
    copies = []
    for k in range(parts):
        at = slice(k * span, (k + 1) * span)
        onehot = jnp.where(box_ids == slots_ref[:, at], 1.0, 0.0).astype(BF16)
        for c in range(channels):
            rows = lax.dot_general(
                onehot, mult_ref[c], (((0,), (1,)), ((), ())), preferred_element_type=F32
            ).astype(BF16)
            rows = jnp.concatenate([rows, jnp.zeros((span, KPAD - points), BF16)], axis=1)
            rows_ref[at, c * KPAD : (c + 1) * KPAD] = rows
        copies.append(pltpu.make_async_copy(rows_ref.at[at], out_hbm.at[at], sem.at[k]))
        copies[k].start()
    for copy in copies:
        copy.wait()


def pack(multipoles, send_slots):
    channels, points, slots = multipoles.shape
    ghosts = send_slots.shape[1]
    half = slots // 2
    return pl.pallas_call(
        pack_kernel,
        grid=(1,),
        in_specs=[
            pl.BlockSpec((channels, points, half), lambda i: (0, 0, 0)),
            pl.BlockSpec((1, ghosts), lambda i: (0, 0)),
        ],
        out_specs=pl.BlockSpec(memory_space=pl.ANY),
        out_shape=jax.ShapeDtypeStruct((ghosts, channels * KPAD), BF16),
        scratch_shapes=[
            pltpu.VMEM((ghosts, channels * KPAD), BF16),
            pltpu.SemaphoreType.DMA((ghosts // 256,)),
        ],
        compiler_params=pltpu.CompilerParams(vmem_limit_bytes=60 * 2**20),
    )(multipoles, send_slots)


def local_kernel(live_ref, mult_ref, out_ref):
    channels, points, slots = mult_ref.shape
    keep = lax.broadcasted_iota(jnp.int32, (slots, 1), 0) < live_ref[0]
    for c in range(channels):
        rows = jnp.where(keep, mult_ref[c].astype(F32).T, 0.0).astype(BF16)
        rows = jnp.concatenate([rows, jnp.zeros((slots, KPAD - points), BF16)], axis=1)
        out_ref[:, c * KPAD : (c + 1) * KPAD] = rows


def local_rows(live, multipoles):
    channels, points, slots = multipoles.shape
    return pl.pallas_call(
        local_kernel,
        in_specs=[
            pl.BlockSpec(memory_space=pltpu.SMEM),
            pl.BlockSpec(memory_space=pltpu.VMEM),
        ],
        out_specs=pl.BlockSpec(memory_space=pltpu.VMEM),
        out_shape=jax.ShapeDtypeStruct((slots, channels * KPAD), BF16),
        compiler_params=pltpu.CompilerParams(vmem_limit_bytes=40 * 2**20),
    )(live, multipoles)


def ops_kernel(t_ref, out_ref):
    points = t_ref.shape[1]
    out_ref[...] = jnp.zeros_like(out_ref)
    for k in range(t_ref.shape[0]):
        out_ref[k, :points, :points] = t_ref[k].astype(F32).T.astype(BF16)


def padded_ops(ops, count):
    rel, points, _ = ops.shape
    return pl.pallas_call(
        ops_kernel,
        grid=(rel // count,),
        in_specs=[pl.BlockSpec((count, points, points), lambda i: (i, 0, 0))],
        out_specs=pl.BlockSpec((count, KPAD, KPAD), lambda i: (i, 0, 0)),
        out_shape=jax.ShapeDtypeStruct((rel, KPAD, KPAD), BF16),
        compiler_params=pltpu.CompilerParams(vmem_limit_bytes=16 * 2**20),
    )(ops)


def m2l_kernel(
    vl_ref, live_ref, arr_hbm, loc_hbm, t_hbm, out_hbm, buf, acc, arr_ref, loc_ref, t_ref, stage, loc_sem, arr_sem, t_sem, out_sem, *, depth, batch
):
    slots = loc_ref.shape[0]
    ghosts = arr_ref.shape[0]
    parts = arr_sem.shape[0]
    span = ghosts // parts
    channels, points, _ = stage.shape
    chunks = KPAD // LANES
    groups = t_hbm.shape[0] // depth
    laps = groups // 2
    first = (slots + ghosts + 4) * BOX

    def start(p):
        return first + p * slots * BOX

    def gather(r, p, t0, t1):
        base = r * slots
        for tb in range(t0, t1, batch):
            held = []
            for t in range(tb, tb + batch):
                i = vl_ref[base + t]
                held.append((start(p) + t * BOX, buf[pl.ds(i, 8), :], buf[pl.ds(i + 8, BOX - 8), :]))
            for to, head, tail in held:
                buf[pl.ds(to, 8), :] = head
                buf[pl.ds(to + 8, BOX - 8), :] = tail

    def ops_copy(lap):
        place = lax.rem(lap, 2)
        return pltpu.make_async_copy(t_hbm.at[pl.ds(lap * 2 * depth, 2 * depth)], t_ref.at[place], t_sem.at[place])

    def part_copy(k):
        rows = pl.ds(k * span, span)
        return pltpu.make_async_copy(arr_hbm.at[rows], arr_ref.at[rows], arr_sem.at[k])

    def fill(ref, low, count, at):
        def one(b, carry):
            rows = ref[pl.ds(pl.multiple_of(low + b * 16, 16), 16), :].astype(F32)
            for q in range(BOX):
                buf[pl.ds((at + b * 16) * BOX + q, 16, stride=BOX), :] = rows[:, q * LANES : (q + 1) * LANES]
            return carry

        lax.fori_loop(0, count // 16, one, 0, unroll=2)

    loc_copy = pltpu.make_async_copy(loc_hbm, loc_ref, loc_sem)
    loc_copy.start()
    for k in range(parts):
        part_copy(k).start()
    ops_copy(0).start()
    acc[...] = jnp.zeros_like(acc)
    loc_copy.wait()
    fill(loc_ref, 0, slots, 0)
    for k in range(parts):
        part_copy(k).wait()
        fill(arr_ref, k * span, span, slots + k * span)
    buf[pl.ds((slots + ghosts) * BOX, 16), :] = jnp.zeros((16, LANES), F32)
    for p in range(depth):
        gather(p, p, 0, slots)

    def group(s, slot, place, last=False):
        later = jnp.minimum(s + 1, groups - 1)
        total = depth * slots
        cuts = [total * c // channels // batch * batch for c in range(channels + 1)]
        def fetch(c):
            for p in range(depth):
                lo, hi = max(cuts[c] - p * slots, 0), min(cuts[c + 1] - p * slots, slots)
                if lo < hi:
                    gather(later * depth + p, (1 - slot) * depth + p, lo, hi)

        def multiply(c):
            x = jnp.concatenate(
                [
                    buf[pl.ds(start(slot * depth + p) + c * chunks + q, slots, stride=BOX), :].astype(BF16)
                    for p in range(depth)
                    for q in range(chunks)
                ],
                axis=1,
            )
            w = t_ref[place, slot * depth : (slot + 1) * depth].reshape(depth * KPAD, KPAD)
            acc[c] += jnp.dot(x, w, preferred_element_type=F32)

        for c in range(channels):
            if not last:
                fetch(c)
            multiply(c)
            if last:
                finish(c)

    keep = lax.broadcasted_iota(jnp.int32, (1, slots), 1) < live_ref[0]

    def out_copy(c):
        return pltpu.make_async_copy(stage.at[c], out_hbm.at[c], out_sem.at[c])

    def finish(c):
        stage[c] = jnp.where(keep, acc[c].T[:points], 0.0)
        out_copy(c).start()

    def lap(s, carry):
        place = lax.rem(s, 2)
        ops_copy(s).wait()
        ops_copy(s + 1).start()
        group(2 * s, 0, place)
        group(2 * s + 1, 1, place)
        return carry

    lax.fori_loop(0, laps - 1, lap, 0)
    end = laps - 1
    ops_copy(end).wait()
    group(2 * end, 0, end % 2)
    group(2 * end + 1, 1, end % 2, last=True)
    for c in range(channels):
        out_copy(c).wait()


def m2l(cols, live, arrived, local, ops, channels, points):
    ghosts = arrived.shape[0]
    slots = local.shape[0]
    depth = 3
    smem = pl.BlockSpec(memory_space=pltpu.SMEM)
    hbm = pl.BlockSpec(memory_space=pl.ANY)
    return pl.pallas_call(
        functools.partial(m2l_kernel, depth=depth, batch=8),
        in_specs=[smem, smem, hbm, hbm, hbm],
        out_specs=hbm,
        scratch_shapes=[
            pltpu.VMEM(((slots + ghosts + 4 + 2 * depth * slots) * BOX, LANES), F32),
            pltpu.VMEM((channels, slots, KPAD), F32),
            pltpu.VMEM(arrived.shape, BF16),
            pltpu.VMEM(local.shape, BF16),
            pltpu.VMEM((2, 2 * depth, KPAD, KPAD), BF16),
            pltpu.VMEM((channels, points, slots), F32),
            pltpu.SemaphoreType.DMA,
            pltpu.SemaphoreType.DMA((4,)),
            pltpu.SemaphoreType.DMA((2,)),
            pltpu.SemaphoreType.DMA((channels,)),
        ],
        out_shape=jax.ShapeDtypeStruct((channels, points, slots), F32),
        compiler_params=pltpu.CompilerParams(vmem_limit_bytes=56 * 2**20),
    )(cols, live, arrived, local, ops)


def shifted(cells, step):
    count = lax.axis_size("morton")
    if step > 0:
        pairs = [(i, i + 1) for i in range(count - 1)]
    else:
        pairs = [(i + 1, i) for i in range(count - 1)]
    return lax.ppermute(cells, "morton", pairs)


def body(multipoles, upward_ops, transfer_ops, live_counts, seam_joins, send_slots, vlist_cols):
    channels, points, slot_total = multipoles.shape
    group_total = slot_total // 8
    dev_count = lax.axis_size("morton")
    ghosts = send_slots.shape[1]
    width = channels * KPAD
    outgoing = pack(multipoles, send_slots)
    outgoing, multipoles, transfer_ops = lax.optimization_barrier((outgoing, multipoles, transfer_ops))
    arrived = lax.all_to_all(
        outgoing.reshape(dev_count, ghosts // dev_count, width), "morton", 0, 0, tiled=True
    ).reshape(ghosts, width)

    local = local_rows(live_counts, multipoles)
    ops = padded_ops(transfer_ops, 2)
    cols = (vlist_cols.T * BOX).reshape(-1)

    slot_ids = jnp.arange(slot_total, dtype=jnp.int32)
    keep = (slot_ids < live_counts[0])[None, None, :]
    masked = jnp.where(keep, multipoles, jnp.zeros_like(multipoles))
    children = masked.reshape(channels, points, group_total, 8)
    partial_value = jnp.einsum("oij,cjgo->cig", upward_ops, children, preferred_element_type=F32)
    last_group = (live_counts[0] - 1) // 8
    last_part = lax.dynamic_slice_in_dim(partial_value, last_group, 1, 2)[:, :, 0]
    from_left = shifted(last_part, 1)
    from_right = shifted(partial_value[:, :, 0], -1)
    group_ids = jnp.arange(group_total, dtype=jnp.int32)
    joins = seam_joins[0].astype(F32)
    parent_mult = partial_value + jnp.where(
        (group_ids == 0)[None, None, :], (joins[0] * from_left)[:, :, None], F32(0.0)
    )
    parent_mult = parent_mult + jnp.where(
        (group_ids == last_group)[None, None, :], (joins[1] * from_right)[:, :, None], F32(0.0)
    )
    local_check = m2l(cols, live_counts, arrived, local, ops, channels, points)
    return (local_check, parent_mult)


def solution(mesh):
    placed = (
        P(None, None, "morton"),
        P(),
        P(),
        P("morton"),
        P("morton", None),
        P("morton", None),
        P("morton", None),
    )
    return jax.shard_map(
        body,
        mesh=mesh,
        in_specs=placed,
        out_specs=(P(None, None, "morton"), P(None, None, "morton")),
        check_vma=False,
    )
```
